32 devices in a mesh: vel: 2 (over y), cell: 16 (over z, x, core).
Axes of the slice: x: 2, y: 2, z: 4, core: 2. Of those that a mesh axis runs over, the one named last changes fastest.
Arguments:
- distribution: float32 [4096, 4096], P('vel', 'cell'), as said below
- cell_count: int32 [16], P('cell'), may hold values from 192 to 256, as said below
- cell_level: int32 [4096], P('cell'), may hold values from 0 to 1
- send_list: int32 [4, 1024], P(None, 'cell'), may hold values from 0 to 255, as said below
- face_neighbour: int32 [6, 4096], P(None, 'cell'), may hold values from 0 to 511, as said below
- face_level: int32 [6, 4096], P(None, 'cell'), may hold values from 0 to 1
Outputs:
- advanced: float32 [4096, 4096], P('vel', 'cell')
The draws below stay inside these ranges and needn't reach their ends.
Inputs may be any that keep to these rules, and one draw needn't show every extreme that they name: The live cells of index d of cell are its slots 0 to cell_count[d] - 1; the rest are padding. Some index has all 256 live. `send_list`: row k of index d lists live local cells of d; the neighbour d + o_k, o = (-2, -1, 1, 2), reads a prefix of the row, and no one reads a row toward an index outside the mesh. Every index has some row whose 64 slots are all read. `face_neighbour`: every entry of a live cell names a live cell: below 256 a local one, else a read slot of a neighbour's send list as in the reference program. `distribution`: positive everywhere.
All inputs are finite; a program needn't handle non-finite values.
Results may differ from the reference program's by a relative error of at most 0.0001.
Values sent between devices are 32-bit elements; how exact they have to be, the bound alone decides.
A program may use at most 64 MiB of HBM per device.

```python
import math
import jax
import jax.numpy as jnp
from jax import lax

NV = 16
CELL_DEV = 256
STEPS = 2
SEND_MAX = 64
V = 4096
CELLS = 4096
N_CELL = 16


def partition_layout(key):
    sampler_seeds = jax.random.split(jax.random.fold_in(key, 101), 9)
    devices = jnp.arange(N_CELL, dtype=jnp.int32)
    counts = jax.random.randint(sampler_seeds[0], (N_CELL,), CELL_DEV * 3 // 4, CELL_DEV + 1)
    fullest = jax.random.randint(sampler_seeds[1], (), 0, N_CELL)
    counts = jnp.where(devices == fullest, CELL_DEV, counts).astype(jnp.int32)
    offsets = jnp.array([-2, -1, 1, 2], dtype=jnp.int32)
    partner = devices[:, None] + offsets[None, :]
    present = (partner >= 0) & (partner < N_CELL)
    lengths = jax.random.randint(sampler_seeds[2], (N_CELL, 4), SEND_MAX // 2, SEND_MAX + 1)
    chosen = jax.random.randint(sampler_seeds[3], (N_CELL,), 0, 4)
    chosen_ok = jnp.take_along_axis(present, chosen[:, None], 1)[:, 0]
    chosen = jnp.where(chosen_ok, chosen, jnp.where(devices > 0, 1, 2))
    lengths = jnp.where(jnp.arange(4)[None, :] == chosen[:, None], SEND_MAX, lengths)
    lengths = jnp.where(jnp.arange(4)[None, :] == 0, SEND_MAX, lengths)
    lengths = jnp.where(present, lengths, 0)
    entries = jax.random.randint(sampler_seeds[4], (N_CELL, 4, SEND_MAX), 0, counts[:, None, None])
    entries = jnp.where(jnp.arange(SEND_MAX)[None, None, :] == 0, counts[:, None, None] - 1, entries)
    used = jnp.arange(SEND_MAX)[None, None, :] < lengths[:, :, None]
    send_rows = jnp.where(used, entries, 0).transpose(1, 0, 2).reshape(4, N_CELL * SEND_MAX)
    source = jnp.clip(partner, 0, N_CELL - 1)
    incoming = jnp.where(present, lengths[source, 3 - jnp.arange(4)[None, :]], 0)
    group_id = jax.random.randint(sampler_seeds[5], (6, N_CELL, CELL_DEV), 0, 4)
    available = jnp.sum(jnp.where(group_id[..., None] == jnp.arange(4), incoming[None, :, None, :], 0), -1)
    slot_id = jax.random.randint(sampler_seeds[6], (6, N_CELL, CELL_DEV), 0, SEND_MAX) % jnp.maximum(available, 1)
    remote = (jax.random.randint(sampler_seeds[7], (6, N_CELL, CELL_DEV), 0, 4) == 0) & (available > 0)
    local = jax.random.randint(sampler_seeds[8], (6, N_CELL, CELL_DEV), 0, counts[None, :, None])
    neighbours = jnp.where(remote, CELL_DEV + group_id * SEND_MAX + slot_id, local)
    face_ids = jnp.arange(6, dtype=jnp.int32)[:, None, None]
    first_cell = jnp.arange(CELL_DEV, dtype=jnp.int32)[None, None, :] == 0
    far_ok = (devices + 2 < N_CELL)[None, :, None]
    neighbours = jnp.where(first_cell & (face_ids == 0), 0, neighbours)
    neighbours = jnp.where(first_cell & (face_ids == 1) & far_ok, CELL_DEV + 4 * SEND_MAX - 1, neighbours)
    neighbours = neighbours.reshape(6, N_CELL * CELL_DEV)
    return (counts, send_rows.astype(jnp.int32), neighbours.astype(jnp.int32))


def draw_cell_count(key, part):
    layout = partition_layout(key)
    return layout[0]


def draw_send_list(key, part):
    layout = partition_layout(key)
    return layout[1]


def draw_face_neighbour(key, part):
    layout = partition_layout(key)
    return layout[2]


def draw_distribution(key, part):
    key = jax.random.fold_in(key, 7)
    sampler_seeds = jax.random.split(key, 5)
    volume_distributions = CELL_DEV * N_CELL
    velocities = NV ** 3
    local_concentration = jnp.exp(jax.random.uniform(sampler_seeds[0], (volume_distributions,), minval=math.log(0.3), maxval=math.log(3.0)))
    kinetic_warmth = jax.random.uniform(sampler_seeds[1], (volume_distributions,), minval=0.5, maxval=2.0)
    drift = jax.random.uniform(sampler_seeds[2], (3, volume_distributions), minval=-1.0, maxval=1.0)
    asymmetry_correction = jax.random.uniform(sampler_seeds[3], (3, volume_distributions), minval=-1.0, maxval=1.0)
    index = jnp.arange(velocities, dtype=jnp.int32)
    spacing = 10.0 / NV
    lattice_nodes_east = (-5.0 + ((index // (NV * NV)).astype(jnp.float32) + 0.5) * spacing)[:, None]
    lattice_nodes_north = (-5.0 + ((index // NV % NV).astype(jnp.float32) + 0.5) * spacing)[:, None]
    lattice_nodes_upward = (-5.0 + ((index % NV).astype(jnp.float32) + 0.5) * spacing)[:, None]
    width_east = lattice_nodes_east - drift[0][None, :]
    width_north = lattice_nodes_north - drift[1][None, :]
    width_upward = lattice_nodes_upward - drift[2][None, :]
    agitation_magnitude = width_east * width_east + width_north * width_north + width_upward * width_upward
    starting_shift_amount = (local_concentration * kinetic_warmth ** (-1.5))[None, :] * jnp.exp(-agitation_magnitude / (2.0 * kinetic_warmth[None, :]))
    inclined_correction = (asymmetry_correction[0][None, :] * width_east + asymmetry_correction[1][None, :] * width_north + asymmetry_correction[2][None, :] * width_upward) / jnp.sqrt(kinetic_warmth)[None, :]
    inclined_correction = inclined_correction * (agitation_magnitude / (2.0 * kinetic_warmth[None, :]) - 2.5) * 0.3
    shaping = 1.0 + 0.5 * jnp.tanh(inclined_correction)
    noise = 1.0 + 0.15 * jnp.clip(jax.random.normal(sampler_seeds[4], (velocities, volume_distributions)), -3.0, 3.0)
    return (starting_shift_amount * shaping * noise).astype(jnp.float32)


def set_ends(values, rng, smallest, high):
    longest = values.shape.index(max(values.shape))
    spots = []
    for shift in (0, 1):
        where = [jax.random.randint(jax.random.fold_in(rng, axis), (), 0, length) for axis, length in enumerate(values.shape)]
        where[longest] = (where[longest] + shift) % values.shape[longest]
        spots.append(tuple(where))
    return values.at[spots[0]].set(smallest).at[spots[1]].set(high)


def setup_inputs(seed: int = 0) -> dict:
    key_list = jax.random.split(jax.random.key(seed), 7)
    distribution = draw_distribution(jax.random.fold_in(key_list[6], 71), 0)
    cell_count = draw_cell_count(jax.random.fold_in(key_list[6], 71), 0)
    cell_level = set_ends(jax.random.randint(key_list[2], (CELLS,), 0, 2), jax.random.fold_in(key_list[2], 1), 0, 1).astype(jnp.int32)
    send_list = draw_send_list(jax.random.fold_in(key_list[6], 71), 0)
    face_neighbour = draw_face_neighbour(jax.random.fold_in(key_list[6], 71), 0)
    face_level = set_ends(jax.random.randint(key_list[5], (6, CELLS), 0, 2), jax.random.fold_in(key_list[5], 1), 0, 1).astype(jnp.int32)
    return dict(distribution=distribution, cell_count=cell_count, cell_level=cell_level, send_list=send_list, face_neighbour=face_neighbour, face_level=face_level)


speed_limit = 5.0
time_step = 0.03
nominal_shear_drag = 0.5
power_law_index = 0.81
conduction_quotient = 2.0 / 3.0


def grid_speeds(count):
    index = jnp.arange(count, dtype=jnp.int32)
    spacing = 2.0 * speed_limit / NV
    first = index // (NV * NV)
    second = (index // NV) % NV
    third = index % NV
    lattice_nodes_east = -speed_limit + (first.astype(jnp.float32) + 0.5) * spacing
    lattice_nodes_north = -speed_limit + (second.astype(jnp.float32) + 0.5) * spacing
    lattice_nodes_upward = -speed_limit + (third.astype(jnp.float32) + 0.5) * spacing
    return lattice_nodes_east[:, None], lattice_nodes_north[:, None], lattice_nodes_upward[:, None]


def quadrature_weight():
    return (2.0 * speed_limit / NV) ** 3 * (2.0 * math.pi) ** -1.5


def face_ratios(cell_level, face_level):
    own_level = cell_level[None, :]
    coarser = jnp.maximum(own_level, face_level)
    return jnp.exp2((3 * own_level - 2 * coarser).astype(jnp.float32))


def invariant_integrals(local_concentration, moment_x, moment_y, moment_z, complete_enthalpy_sum, occupied_flags):
    safe_positive_entry = jnp.where(occupied_flags, local_concentration, 1.0)
    mean_flow_east = moment_x / safe_positive_entry
    mean_flow_north = moment_y / safe_positive_entry
    mean_flow_upward = moment_z / safe_positive_entry
    kinetic_warmth = jnp.where(occupied_flags, (complete_enthalpy_sum / safe_positive_entry - (mean_flow_east * mean_flow_east + mean_flow_north * mean_flow_north + mean_flow_upward * mean_flow_upward)) / 3.0, 1.0)
    return safe_positive_entry, mean_flow_east, mean_flow_north, mean_flow_upward, kinetic_warmth


def corrected_profile(lattice_nodes_east, lattice_nodes_north, lattice_nodes_upward, local_concentration, mean_flow_vectors, kinetic_warmth, isotropic_stress, conduction_vectors):
    width_east = lattice_nodes_east - mean_flow_vectors[0][None, :]
    width_north = lattice_nodes_north - mean_flow_vectors[1][None, :]
    width_upward = lattice_nodes_upward - mean_flow_vectors[2][None, :]
    agitation_magnitude = width_east * width_east + width_north * width_north + width_upward * width_upward
    gaussian_profile = (local_concentration * kinetic_warmth ** -1.5)[None, :] * jnp.exp(-agitation_magnitude / (2.0 * kinetic_warmth[None, :]))
    coordinate_location = width_east * conduction_vectors[0][None, :] + width_north * conduction_vectors[1][None, :] + width_upward * conduction_vectors[2][None, :]
    multiplier_coefficient = (1.0 - conduction_quotient) / (5.0 * isotropic_stress * kinetic_warmth)
    return gaussian_profile * (1.0 + multiplier_coefficient[None, :] * coordinate_location * (agitation_magnitude / kinetic_warmth[None, :] - 5.0))


def heat_terms(leaf_volumes, lattice_nodes_east, lattice_nodes_north, lattice_nodes_upward, mean_flow_vectors):
    width_east = lattice_nodes_east - mean_flow_vectors[0][None, :]
    width_north = lattice_nodes_north - mean_flow_vectors[1][None, :]
    width_upward = lattice_nodes_upward - mean_flow_vectors[2][None, :]
    scaled = (0.5 * quadrature_weight()) * (width_east * width_east + width_north * width_north + width_upward * width_upward) * leaf_volumes
    return jnp.stack([jnp.sum(width_east * scaled, 0), jnp.sum(width_north * scaled, 0), jnp.sum(width_upward * scaled, 0)])


def march_leaf_volumes(leaf_volumes, lattice_nodes_east, lattice_nodes_north, lattice_nodes_upward, local_concentration, mean_flow_vectors, kinetic_warmth, isotropic_stress, conduction_vectors, inverse_relax_time, attractor_profiles, normalized_peculiar, occupied_flags):
    balance_profile = corrected_profile(lattice_nodes_east, lattice_nodes_north, lattice_nodes_upward, local_concentration, mean_flow_vectors, kinetic_warmth, isotropic_stress, conduction_vectors)
    flux = jnp.zeros_like(leaf_volumes)
    speeds = (lattice_nodes_east, lattice_nodes_north, lattice_nodes_upward)
    for face_slot in range(6):
        normal = speeds[face_slot // 2] * (1.0 - 2.0 * (face_slot % 2))
        across = jnp.take(leaf_volumes, attractor_profiles[face_slot], axis=1)
        flux = flux + normalized_peculiar[face_slot][None, :] * (jnp.maximum(normal, 0.0) * leaf_volumes + jnp.minimum(normal, 0.0) * across)
    refreshed_distribution = leaf_volumes - time_step * flux + time_step * inverse_relax_time[None, :] * (balance_profile - leaf_volumes)
    return jnp.where(occupied_flags[None, :], refreshed_distribution, 0.0)


def global_neighbours(device, send_list, face_neighbour):
    ghost = face_neighbour >= CELL_DEV
    offset_slot = jnp.maximum(face_neighbour - CELL_DEV, 0)
    group_id = offset_slot // SEND_MAX
    slot_id = offset_slot % SEND_MAX
    offsets = jnp.array([-2, -1, 1, 2], dtype=jnp.int32)
    source = jnp.clip(device[None, :] + offsets[group_id], 0, N_CELL - 1)
    listed = send_list[3 - group_id, source * SEND_MAX + slot_id]
    return jnp.where(ghost, source * CELL_DEV + listed, device[None, :] * CELL_DEV + face_neighbour).astype(jnp.int32)


def reference(distribution, cell_count, cell_level, send_list, face_neighbour, face_level):
    cell_index = jnp.arange(CELLS, dtype=jnp.int32)
    device = cell_index // CELL_DEV
    occupied_flags = (cell_index % CELL_DEV) < cell_count[device]
    attractor_profiles = global_neighbours(device, send_list, face_neighbour)
    normalized_peculiar = face_ratios(cell_level, face_level)
    lattice_nodes_east, lattice_nodes_north, lattice_nodes_upward = grid_speeds(V)
    quadrature = quadrature_weight()
    block_rows = min(V, 512)
    block_count = V // block_rows
    donor_transport_east = lattice_nodes_east.reshape(block_count, block_rows, 1)
    donor_transport_north = lattice_nodes_north.reshape(block_count, block_rows, 1)
    donor_transport_upward = lattice_nodes_upward.reshape(block_count, block_rows, 1)
    squared = lattice_nodes_east * lattice_nodes_east + lattice_nodes_north * lattice_nodes_north + lattice_nodes_upward * lattice_nodes_upward
    matrix = quadrature * jnp.concatenate([jnp.ones_like(lattice_nodes_east), lattice_nodes_east, lattice_nodes_north, lattice_nodes_upward, squared], axis=1).T
    state_values = distribution
    for step_number in range(STEPS):
        integral_sums = jnp.dot(matrix, state_values, precision=lax.Precision.HIGHEST)
        safe_positive_entry, mean_flow_east, mean_flow_north, mean_flow_upward, kinetic_warmth = invariant_integrals(integral_sums[0], integral_sums[1], integral_sums[2], integral_sums[3], integral_sums[4], occupied_flags)
        mean_flow_vectors = (mean_flow_east, mean_flow_north, mean_flow_upward)
        regrouped_distribution = state_values.reshape(block_count, block_rows, CELLS)
        conduction_vectors = jnp.sum(lax.map(lambda integral_parts: heat_terms(integral_parts[0], integral_parts[1], integral_parts[2], integral_parts[3], mean_flow_vectors), (regrouped_distribution, donor_transport_east, donor_transport_north, donor_transport_upward)), 0)
        isotropic_stress = safe_positive_entry * kinetic_warmth
        inverse_relax_time = isotropic_stress / (nominal_shear_drag * kinetic_warmth ** power_law_index)
        local_concentration = integral_sums[0]
        refreshed_distribution = lax.map(lambda integral_parts: march_leaf_volumes(integral_parts[0], integral_parts[1], integral_parts[2], integral_parts[3], local_concentration, mean_flow_vectors, kinetic_warmth, isotropic_stress, (conduction_vectors[0], conduction_vectors[1], conduction_vectors[2]), inverse_relax_time, attractor_profiles, normalized_peculiar, occupied_flags), (regrouped_distribution, donor_transport_east, donor_transport_north, donor_transport_upward))
        state_values = refreshed_distribution.reshape(V, CELLS)
    return state_values
```

```python
import functools
import math

import jax
import jax.numpy as jnp
from jax import lax
from jax.experimental import pallas as pl
from jax.experimental.pallas import tpu as pltpu
from jax.sharding import PartitionSpec as P

NV = 16
STEPS = 2
SPEED_LIMIT = 5.0
SPACING = 2.0 * SPEED_LIMIT / NV
DT = 0.03
DRAG = 0.5
POWER = 0.81
PRANDTL_TERM = 1.0 - 2.0 / 3.0
WEIGHT = SPACING**3 * (2.0 * math.pi) ** (-1.5)
OFFSETS = (-2, -1, 1, 2)
F32 = jnp.float32
BF16 = jnp.bfloat16


def node(index):
    return -SPEED_LIMIT + (index + 0.5) * SPACING


def split(values):
    high = values.astype(BF16)
    return high, (values - high.astype(F32)).astype(BF16)


def kernel(
    n_cell, n_vel, planes,
    dist, count, level, sends, faces, face_level, out,
    state1, send_buf, recv_buf, pick, move, acc, part, parts, b_terms, e_terms, c_terms, ratios,
    send_sem, recv_sem, part_send, part_recv,
):
    d = lax.axis_index("cell")
    vel = lax.axis_index("vel")
    first_a = vel * planes
    there = [jnp.logical_and(d + o >= 0, d + o < n_cell) for o in OFFSETS]
    live = lax.broadcasted_iota(jnp.int32, (8, 256), 1) < count[0]
    low_lanes = lax.broadcasted_iota(jnp.int32, (128, 128), 1) < 64

    barrier = pltpu.get_barrier_semaphore()
    for j, o in enumerate(OFFSETS):
        @pl.when(there[j])
        def _(o=o):
            pl.semaphore_signal(barrier, inc=1, device_id={"cell": d + o})
    for k in range(1, n_vel):
        pl.semaphore_signal(barrier, inc=1, device_id={"vel": lax.rem(vel + k, n_vel)})

    cells = lax.broadcasted_iota(jnp.int32, (256, 256), 0)
    pick[...] = jnp.where(cells == sends[...], 1.0, 0.0).astype(BF16)
    own = level[...]
    ratio = jnp.exp2((3 * own - 2 * jnp.maximum(own, face_level[...])).astype(F32))
    columns = lax.broadcasted_iota(jnp.int32, (512, 256), 0)
    west = first_a < NV // 2
    in_x = jnp.where(west, faces[0:1], faces[1:2])
    ratio_in = jnp.where(west, ratio[0:1], ratio[1:2])
    ratio_out = jnp.where(west, ratio[1:2], ratio[0:1])
    move[0] = jnp.where(columns == in_x, ratio_in, 0.0).astype(BF16)
    for k in range(2, 6):
        move[k - 1] = jnp.where(columns == faces[k:k + 1], ratio[k:k + 1], 0.0).astype(BF16)
        ratios[k] = jnp.broadcast_to(ratio[k:k + 1], (8, 256))
    ratios[0] = jnp.broadcast_to(ratio_out, (8, 256))

    pl.semaphore_wait(barrier, n_vel - 1 + sum(t.astype(jnp.int32) for t in there))
    for j in range(4):
        @pl.when(jnp.logical_not(there[j]))
        def _(j=j):
            for s in range(STEPS):
                def clear(p, carry):
                    recv_buf[s, p, j] = jnp.zeros((128, 128), F32)
                    return carry
                lax.fori_loop(0, planes, clear, 0)

    def message(s, p, j):
        return pltpu.make_async_remote_copy(
            src_ref=send_buf.at[s, p, j],
            dst_ref=recv_buf.at[s, p, 3 - j],
            send_sem=send_sem.at[s, p, j],
            recv_sem=recv_sem.at[s, p, 3 - j],
            device_id={"cell": d + OFFSETS[j]},
        )

    def send_plane(s, p, high, low):
        both = jnp.dot(jnp.concatenate([high, low], 0), pick[...], preferred_element_type=F32)
        packed = both[:256] + both[256:]
        for pair in range(2):
            upper = packed[:128, pair * 128:pair * 128 + 128]
            lower = packed[128:, pair * 128:pair * 128 + 128]
            send_buf[s, p, 2 * pair] = jnp.where(low_lanes, upper, pltpu.roll(lower, 64, 1))
            send_buf[s, p, 2 * pair + 1] = jnp.where(low_lanes, pltpu.roll(upper, 64, 1), lower)
        for j in range(4):
            @pl.when(there[j])
            def _(j=j):
                message(s, p, j).start()

    def add_moments(p, plane):
        c = node((first_a + p).astype(F32))
        acc[0] += plane
        acc[1] += c * plane
        acc[2] += (c * c) * plane
        acc[3] += (c * c * c) * plane

    def finish_moments(s):
        nodes = [node(lax.broadcasted_iota(jnp.int32, (8, 256), 0).astype(F32) + 8.0 * eh) for eh in range(2)]
        u = {}
        for q in range(4):
            for r in range(4 - q):
                for eh in range(2):
                    total = None
                    for b in range(NV):
                        row = acc[q, pl.ds(eh * 128 + b * 8, 8), :]
                        term = row if r == 0 else row * (node(b) ** r)
                        total = term if total is None else total + term
                    u[q, r, eh] = total

        def moment(q, r, t):
            value = 0.0
            for eh in range(2):
                term = u[q, r, eh]
                for _ in range(t):
                    term = term * nodes[eh]
                value = value + term
            return value

        rows = [
            moment(0, 0, 0), moment(1, 0, 0), moment(0, 1, 0), moment(0, 0, 1),
            moment(2, 0, 0), moment(0, 2, 0), moment(0, 0, 2),
            moment(1, 1, 0), moment(1, 0, 1), moment(0, 1, 1),
            moment(3, 0, 0) + moment(1, 2, 0) + moment(1, 0, 2),
            moment(2, 1, 0) + moment(0, 3, 0) + moment(0, 1, 2),
            moment(2, 0, 1) + moment(0, 2, 1) + moment(0, 0, 3),
        ]
        for i, value in enumerate(rows):
            part[s, i:i + 1] = WEIGHT * jnp.sum(value, 0, keepdims=True)
        part[s, 13:16] = jnp.zeros((3, 256), F32)
        copies = []
        for k in range(1, n_vel):
            copies.append(pltpu.make_async_remote_copy(
                src_ref=part.at[s], dst_ref=parts.at[s, k],
                send_sem=part_send.at[s, k], recv_sem=part_recv.at[s, k],
                device_id={"vel": lax.rem(vel + k, n_vel)},
            ))
        for copy in copies:
            copy.start()
        for copy in copies:
            copy.wait()
        total = part[s]
        for k in range(1, n_vel):
            total = total + parts[s, k]
        m = [jnp.broadcast_to(total[i:i + 1], (8, 256)) for i in range(13)]
        density = m[0]
        safe = jnp.where(live, density, 1.0)
        mean = [m[i] / safe for i in (1, 2, 3)]
        energy = m[4] + m[5] + m[6]
        speed = mean[0] * mean[0] + mean[1] * mean[1] + mean[2] * mean[2]
        temperature = jnp.where(live, (energy / safe - speed) / 3.0, 1.0)
        second = ((m[4], m[7], m[8]), (m[7], m[5], m[9]), (m[8], m[9], m[6]))
        along = mean[0] * m[1] + mean[1] * m[2] + mean[2] * m[3]
        heat = []
        for i in range(3):
            cross = sum(mean[k] * second[i][k] for k in range(3))
            heat.append(0.5 * (
                m[10 + i] - 2.0 * cross + speed * m[1 + i]
                - mean[i] * (energy - 2.0 * along + speed * density)
            ))
        pressure = safe * temperature
        log_t = jnp.log(temperature)
        rate = pressure / (DRAG * jnp.exp(POWER * log_t))
        inverse = 1.0 / temperature
        factor = PRANDTL_TERM / (5.0 * pressure * temperature)
        c_terms[0] = mean[0]
        c_terms[1] = inverse
        c_terms[2] = factor * heat[0]
        c_terms[3] = DT * rate * density * jnp.exp(-1.5 * log_t)
        c_terms[4] = 1.0 - DT * rate
        for b in range(NV):
            c = node(b)
            width = c - mean[1]
            square = width * width * inverse
            at = pl.ds(b * 8, 8)
            b_terms[0, at, :] = jnp.exp(-0.5 * square)
            b_terms[1, at, :] = factor * heat[1] * width
            b_terms[2, at, :] = square
            b_terms[3, at, :] = (DT * abs(c)) * ratios[3 if c < 0 else 2]
        for eh in range(2):
            width = nodes[eh] - mean[2]
            square = width * width * inverse
            e_terms[0, eh] = jnp.exp(-0.5 * square)
            e_terms[1, eh] = factor * heat[2] * width
            e_terms[2, eh] = square - 5.0
            e_terms[3, eh] = (DT * jnp.abs(nodes[eh])) * ratios[5 if eh == 0 else 4]

    def advance_plane(s, p, plane):
        for g in range(4):
            @pl.when(there[g])
            def _(g=g):
                pltpu.make_async_remote_copy(
                    src_ref=send_buf.at[s, p, g], dst_ref=recv_buf.at[s, p, g],
                    send_sem=send_sem.at[s, p, g], recv_sem=recv_sem.at[s, p, g],
                    device_id={"cell": d + OFFSETS[g]},
                ).wait_recv()
        pieces = [plane]
        for pair in range(2):
            first, second = recv_buf[s, p, 2 * pair], recv_buf[s, p, 2 * pair + 1]
            pieces.append(jnp.concatenate([
                jnp.where(low_lanes, first, pltpu.roll(second, 64, 1)),
                jnp.where(low_lanes, pltpu.roll(first, 64, 1), second),
            ], 0))
        high, low = split(jnp.concatenate(pieces, 1))

        def across(k, spans):
            left = jnp.concatenate([h[i:j] for h in (high, low) for i, j in spans], 0)
            both = jnp.dot(left, move[k], preferred_element_type=F32)
            half = both.shape[0] // 2
            return both[:half] + both[half:]

        xs = across(0, [(0, 256)])
        ys = [across(1, [(0, 64), (128, 192)]), across(2, [(64, 128), (192, 256)])]
        zs = [across(3, [(0, 128)]), across(4, [(128, 256)])]
        c = node((first_a + p).astype(F32))
        speed = DT * jnp.abs(c)
        width = c - c_terms[0]
        square = width * width * c_terms[1]
        a_gauss = c_terms[3] * jnp.exp(-0.5 * square)
        a_heat = c_terms[2] * width
        a_keep = c_terms[4] - speed * ratios[0]
        rows = []
        for eh in range(2):
            e_node = node(lax.broadcasted_iota(jnp.int32, (8, 256), 0).astype(F32) + 8.0 * eh)
            e_speed = DT * jnp.abs(e_node)
            gauss = a_gauss * e_terms[0, eh]
            warm = a_heat + e_terms[1, eh]
            shape = square + e_terms[2, eh]
            keep = a_keep - e_terms[3, eh]
            for b in range(NV):
                at = eh * 128 + b * 8
                bs = pl.ds(b * 8, 8)
                iy = (b % 8) * 8 + 64 * eh
                f = plane[at:at + 8]
                shakhov = gauss * b_terms[0, bs, :] * (
                    1.0 + (warm + b_terms[1, bs, :]) * (shape + b_terms[2, bs, :])
                )
                new = f * (keep - b_terms[3, bs, :]) + shakhov
                new = new + speed * xs[at:at + 8]
                new = new + (DT * abs(node(b))) * ys[b // 8][iy:iy + 8]
                new = new + e_speed * zs[eh][b * 8:b * 8 + 8]
                rows.append(jnp.where(live, new, 0.0))
        return jnp.concatenate(rows, 0)

    def load_plane(p):
        return jnp.concatenate([dist[p, :, eh].reshape(128, 256) for eh in range(2)], 0)

    def first_send(p, carry):
        high, low = split(load_plane(p))
        send_plane(0, p, high, low)
        return carry

    lax.fori_loop(0, planes, first_send, 0)
    acc[...] = jnp.zeros_like(acc)

    def first_moments(p, carry):
        add_moments(p, load_plane(p))
        return carry

    lax.fori_loop(0, planes, first_moments, 0)
    finish_moments(0)
    acc[...] = jnp.zeros_like(acc)

    def first_step(p, carry):
        new = advance_plane(0, p, load_plane(p))
        high, low = split(new)
        send_plane(1, p, high, low)
        state1[p] = new
        add_moments(p, new)
        return carry

    lax.fori_loop(0, planes, first_step, 0)
    finish_moments(1)

    def second_step(p, carry):
        new = advance_plane(1, p, state1[p])
        for eh in range(2):
            out[p, :, eh] = new[eh * 128:eh * 128 + 128].reshape(16, 8, 256)
        return carry

    lax.fori_loop(0, planes, second_step, 0)

    def drain(p, carry):
        for s in range(STEPS):
            for j in range(4):
                @pl.when(there[j])
                def _(s=s, j=j):
                    message(s, p, j).wait_send()
        return carry

    lax.fori_loop(0, planes, drain, 0)


def solution(mesh):
    n_cell, n_vel = mesh.shape["cell"], mesh.shape["vel"]

    def body(distribution, cell_count, cell_level, send_list, face_neighbour, face_level):
        rows, width = distribution.shape
        planes = rows // (NV * NV)
        shape = (planes, NV, 2, NV // 2, width)
        vmem = pl.BlockSpec(memory_space=pltpu.VMEM)
        result = pl.pallas_call(
            functools.partial(kernel, n_cell, n_vel, planes),
            out_shape=jax.ShapeDtypeStruct(shape, F32),
            in_specs=[vmem, pl.BlockSpec(memory_space=pltpu.SMEM), vmem, vmem, vmem, vmem],
            out_specs=vmem,
            scratch_shapes=[
                pltpu.VMEM((planes, 256, 256), F32),
                pltpu.VMEM((STEPS, planes, 4, 128, 128), F32),
                pltpu.VMEM((STEPS, planes, 4, 128, 128), F32),
                pltpu.VMEM((256, 256), BF16),
                pltpu.VMEM((5, 512, 256), BF16),
                pltpu.VMEM((4, 256, 256), F32),
                pltpu.VMEM((STEPS, 16, 256), F32),
                pltpu.VMEM((STEPS, n_vel, 16, 256), F32),
                pltpu.VMEM((4, 128, 256), F32),
                pltpu.VMEM((4, 2, 8, 256), F32),
                pltpu.VMEM((5, 8, 256), F32),
                pltpu.VMEM((6, 8, 256), F32),
                pltpu.SemaphoreType.DMA((STEPS, planes, 4)),
                pltpu.SemaphoreType.DMA((STEPS, planes, 4)),
                pltpu.SemaphoreType.DMA((STEPS, n_vel)),
                pltpu.SemaphoreType.DMA((STEPS, n_vel)),
            ],
            compiler_params=pltpu.CompilerParams(
                collective_id=0, has_side_effects=True, vmem_limit_bytes=48 * 2**20
            ),
        )(
            distribution.reshape(shape),
            cell_count,
            cell_level.reshape(1, width),
            send_list.reshape(1, width),
            face_neighbour,
            face_level,
        )
        return result.reshape(rows, width)

    placed = (P("vel", "cell"), P("cell"), P("cell"), P(None, "cell"), P(None, "cell"), P(None, "cell"))
    return jax.shard_map(body, mesh=mesh, in_specs=placed, out_specs=P("vel", "cell"), check_vma=False)
```

```python
import functools
import math

import jax
import jax.numpy as jnp
from jax import lax
from jax.experimental import pallas as pl
from jax.experimental.pallas import tpu as pltpu
from jax.sharding import PartitionSpec as P

NV = 16
STEPS = 2
SPEED_LIMIT = 5.0
SPACING = 2.0 * SPEED_LIMIT / NV
DT = 0.03
DRAG = 0.5
POWER = 0.81
PRANDTL_TERM = 1.0 - 2.0 / 3.0
WEIGHT = SPACING**3 * (2.0 * math.pi) ** (-1.5)
OFFSETS = (-2, -1, 1, 2)
F32 = jnp.float32
BF16 = jnp.bfloat16


def node(index):
    return -SPEED_LIMIT + (index + 0.5) * SPACING


def split(values):
    high = values.astype(BF16)
    return high, (values - high.astype(F32)).astype(BF16)


def kernel(
    n_cell, n_vel, planes,
    dist, meta_in, out,
    meta, bulk, out_buf, state1, send_buf, recv_buf, pick, move, acc, part, parts,
    b_terms, e_terms, c_terms, ratios,
    send_sem, recv_sem, part_send, part_recv, bulk_send, bulk_recv, out_send, out_recv, meta_send, meta_recv,
):
    half = planes // 2
    d = lax.axis_index("cell")
    vel = lax.axis_index("vel")
    group = d // 4
    x = (d // 2) % 2
    core = d % 2
    other = 1 - x
    partner = d + 2 - 4 * x
    base = vel * planes
    first_a = base + x * half
    low_lanes = lax.broadcasted_iota(jnp.int32, (128, 128), 1) < 64
    below = group > 0
    above = group < n_cell // 4 - 1

    barrier = pltpu.get_barrier_semaphore()
    pl.semaphore_signal(barrier, inc=1, device_id={"cell": d + 1 - 2 * core})

    @pl.when(below)
    def _():
        pl.semaphore_signal(barrier, inc=1, device_id={"cell": d - 4})

    @pl.when(jnp.logical_and(below, core == 0))
    def _():
        pl.semaphore_signal(barrier, inc=1, device_id={"cell": d - 3})

    @pl.when(above)
    def _():
        pl.semaphore_signal(barrier, inc=1, device_id={"cell": d + 4})

    @pl.when(jnp.logical_and(above, core == 1))
    def _():
        pl.semaphore_signal(barrier, inc=1, device_id={"cell": d + 3})

    def peer(k):
        return {"cell": d if k < n_vel else partner, "vel": lax.rem(vel + k % n_vel, n_vel)}

    for k in range(1, 2 * n_vel):
        pl.semaphore_signal(barrier, inc=1, device_id=peer(k))
    is_below, is_above = below.astype(jnp.int32), above.astype(jnp.int32)
    pl.semaphore_wait(barrier, 2 * n_vel + is_below * (2 - core) + is_above * (1 + core))

    meta_copy = pltpu.make_async_remote_copy(
        src_ref=meta_in, dst_ref=meta.at[x], send_sem=meta_send, recv_sem=meta_recv,
        device_id={"cell": partner},
    )
    meta_copy.start()

    def bulk_copy(p):
        return pltpu.make_async_remote_copy(
            src_ref=dist.at[other * half + p], dst_ref=bulk.at[p],
            send_sem=bulk_send.at[p], recv_sem=bulk_recv.at[p], device_id={"cell": partner},
        )

    def out_copy(p):
        return pltpu.make_async_remote_copy(
            src_ref=out_buf.at[p], dst_ref=out.at[x * half + p],
            send_sem=out_send.at[p], recv_sem=out_recv.at[p], device_id={"cell": partner},
        )

    bulk_copy(0).start()

    def live_cells(t):
        return lax.broadcasted_iota(jnp.int32, (8, 256), 1) < meta[t, 14:15]

    def matrices(t):
        cells = lax.broadcasted_iota(jnp.int32, (256, 256), 0)
        pick[t] = jnp.where(cells == meta[t, 13:14], 1.0, 0.0).astype(BF16)
        own = meta[t, 12:13]
        ratio = jnp.exp2((3 * own - 2 * jnp.maximum(own, meta[t, 6:12])).astype(F32))
        faces = meta[t, 0:6]
        columns = lax.broadcasted_iota(jnp.int32, (512, 256), 0)
        west = base < NV // 2
        in_x = jnp.where(west, faces[0:1], faces[1:2])
        ratio_in = jnp.where(west, ratio[0:1], ratio[1:2])
        ratio_out = jnp.where(west, ratio[1:2], ratio[0:1])
        move[t, 0] = jnp.where(columns == in_x, ratio_in, 0.0).astype(BF16)
        for k in range(2, 6):
            move[t, k - 1] = jnp.where(columns == faces[k:k + 1], ratio[k:k + 1], 0.0).astype(BF16)
            ratios[t, k] = jnp.broadcast_to(ratio[k:k + 1], (8, 256))
        ratios[t, 0] = jnp.broadcast_to(ratio_out, (8, 256))

    def block(t, o):
        there = 4 * group + 2 * t + core + o
        inside = jnp.logical_and(there >= 0, there < n_cell)
        there = jnp.clip(there, 0, n_cell - 1)
        return inside, 4 * (there // 4) + 2 * x + there % 2, (there // 2) % 2

    def is_local(t, j):
        return {0: t == 1, 3: t == 0}.get(j)

    def remote(t, j):
        inside, _, _ = block(t, OFFSETS[j])
        local = is_local(t, j)
        return inside if local is None else jnp.logical_and(inside, jnp.logical_not(local))

    def message(s, t, p, j):
        _, device, place = block(t, OFFSETS[j])
        return pltpu.make_async_remote_copy(
            src_ref=send_buf.at[s, t, p, j],
            dst_ref=recv_buf.at[s, place, p, 3 - j],
            send_sem=send_sem.at[s, t, p, j],
            recv_sem=recv_sem.at[s, place, p, 3 - j],
            device_id={"cell": device},
        )

    def send_plane(s, t, p, plane):
        high, low = split(plane)
        both = jnp.dot(jnp.concatenate([high, low], 0), pick[t], preferred_element_type=F32)
        packed = both[:256] + both[256:]
        values = []
        for pair in range(2):
            upper = packed[:128, pair * 128:pair * 128 + 128]
            lower = packed[128:, pair * 128:pair * 128 + 128]
            values.append(jnp.where(low_lanes, upper, pltpu.roll(lower, 64, 1)))
            values.append(jnp.where(low_lanes, pltpu.roll(upper, 64, 1), lower))
        for j in range(4):
            @pl.when(remote(t, j))
            def _(j=j):
                send_buf[s, t, p, j] = values[j]
                message(s, t, p, j).start()
            if j in (0, 3):
                @pl.when(is_local(t, j))
                def _(j=j):
                    recv_buf[s, 1 - t, p, 3 - j] = values[j]

    def add_moments(t, a, plane):
        c = node(a.astype(F32))
        acc[t, 0] += plane
        acc[t, 1] += c * plane
        acc[t, 2] += (c * c) * plane
        acc[t, 3] += (c * c * c) * plane

    nodes = [node(lax.broadcasted_iota(jnp.int32, (8, 256), 0).astype(F32) + 8.0 * eh) for eh in range(2)]

    def reduce_moments(s, t):
        u = {}
        for q in range(4):
            for r in range(4 - q):
                for eh in range(2):
                    total = None
                    for b in range(NV):
                        row = acc[t, q, pl.ds(eh * 128 + b * 8, 8), :]
                        term = row if r == 0 else row * (node(b) ** r)
                        total = term if total is None else total + term
                    u[q, r, eh] = total

        def moment(q, r, e):
            value = 0.0
            for eh in range(2):
                term = u[q, r, eh]
                for _ in range(e):
                    term = term * nodes[eh]
                value = value + term
            return value

        rows = [
            moment(0, 0, 0), moment(1, 0, 0), moment(0, 1, 0), moment(0, 0, 1),
            moment(2, 0, 0), moment(0, 2, 0), moment(0, 0, 2),
            moment(1, 1, 0), moment(1, 0, 1), moment(0, 1, 1),
            moment(3, 0, 0) + moment(1, 2, 0) + moment(1, 0, 2),
            moment(2, 1, 0) + moment(0, 3, 0) + moment(0, 1, 2),
            moment(2, 0, 1) + moment(0, 2, 1) + moment(0, 0, 3),
        ]
        sums = [WEIGHT * jnp.sum(value, 0, keepdims=True) for value in rows]
        part[s, t] = jnp.concatenate(sums + [jnp.zeros((3, 256), F32)], 0)

    def part_copy(s, k):
        return pltpu.make_async_remote_copy(
            src_ref=part.at[s], dst_ref=parts.at[s, k],
            send_sem=part_send.at[s, k], recv_sem=part_recv.at[s, k], device_id=peer(k),
        )

    def terms(s, t):
        live = live_cells(t)
        total = part[s, t]
        for k in range(1, 2 * n_vel):
            total = total + parts[s, k, t]
        m = [jnp.broadcast_to(total[i:i + 1], (8, 256)) for i in range(13)]
        density = m[0]
        safe = jnp.where(live, density, 1.0)
        mean = [m[i] / safe for i in (1, 2, 3)]
        energy = m[4] + m[5] + m[6]
        speed = mean[0] * mean[0] + mean[1] * mean[1] + mean[2] * mean[2]
        temperature = jnp.where(live, (energy / safe - speed) / 3.0, 1.0)
        second = ((m[4], m[7], m[8]), (m[7], m[5], m[9]), (m[8], m[9], m[6]))
        along = mean[0] * m[1] + mean[1] * m[2] + mean[2] * m[3]
        heat = []
        for i in range(3):
            cross = sum(mean[k] * second[i][k] for k in range(3))
            heat.append(0.5 * (
                m[10 + i] - 2.0 * cross + speed * m[1 + i]
                - mean[i] * (energy - 2.0 * along + speed * density)
            ))
        pressure = safe * temperature
        log_t = jnp.log(temperature)
        rate = pressure / (DRAG * jnp.exp(POWER * log_t))
        inverse = 1.0 / temperature
        factor = PRANDTL_TERM / (5.0 * pressure * temperature)
        c_terms[t, 0] = mean[0]
        c_terms[t, 1] = inverse
        c_terms[t, 2] = factor * heat[0]
        c_terms[t, 3] = DT * rate * density * jnp.exp(-1.5 * log_t)
        c_terms[t, 4] = 1.0 - DT * rate
        for b in range(NV):
            c = node(b)
            width = c - mean[1]
            square = width * width * inverse
            at = pl.ds(b * 8, 8)
            b_terms[t, 0, at, :] = jnp.exp(-0.5 * square)
            b_terms[t, 1, at, :] = factor * heat[1] * width
            b_terms[t, 2, at, :] = square
            b_terms[t, 3, at, :] = (DT * abs(c)) * ratios[t, 3 if c < 0 else 2]
        for eh in range(2):
            width = nodes[eh] - mean[2]
            square = width * width * inverse
            e_terms[t, 0, eh] = jnp.exp(-0.5 * square)
            e_terms[t, 1, eh] = factor * heat[2] * width
            e_terms[t, 2, eh] = square - 5.0
            e_terms[t, 3, eh] = (DT * jnp.abs(nodes[eh])) * ratios[t, 5 if eh == 0 else 4]

    def advance_plane(s, t, p, plane):
        for g in range(4):
            @pl.when(remote(t, g))
            def _(g=g):
                _, device, _ = block(t, OFFSETS[g])
                pltpu.make_async_remote_copy(
                    src_ref=send_buf.at[s, t, p, g], dst_ref=recv_buf.at[s, t, p, g],
                    send_sem=send_sem.at[s, t, p, g], recv_sem=recv_sem.at[s, t, p, g],
                    device_id={"cell": device},
                ).wait_recv()
        pieces = [plane]
        for pair in range(2):
            first, second = recv_buf[s, t, p, 2 * pair], recv_buf[s, t, p, 2 * pair + 1]
            pieces.append(jnp.concatenate([
                jnp.where(low_lanes, first, pltpu.roll(second, 64, 1)),
                jnp.where(low_lanes, pltpu.roll(first, 64, 1), second),
            ], 0))
        high, low = split(jnp.concatenate(pieces, 1))

        def across(k, spans):
            left = jnp.concatenate([h[i:j] for h in (high, low) for i, j in spans], 0)
            both = jnp.dot(left, move[t, k], preferred_element_type=F32)
            size = both.shape[0] // 2
            return both[:size] + both[size:]

        xs = across(0, [(0, 256)])
        ys = [across(1, [(0, 64), (128, 192)]), across(2, [(64, 128), (192, 256)])]
        zs = [across(3, [(0, 128)]), across(4, [(128, 256)])]
        live = live_cells(t)
        c = node((first_a + p).astype(F32))
        speed = DT * jnp.abs(c)
        width = c - c_terms[t, 0]
        square = width * width * c_terms[t, 1]
        a_gauss = c_terms[t, 3] * jnp.exp(-0.5 * square)
        a_heat = c_terms[t, 2] * width
        a_keep = c_terms[t, 4] - speed * ratios[t, 0]
        rows = []
        for eh in range(2):
            e_speed = DT * jnp.abs(nodes[eh])
            gauss = a_gauss * e_terms[t, 0, eh]
            warm = a_heat + e_terms[t, 1, eh]
            shape = square + e_terms[t, 2, eh]
            keep = a_keep - e_terms[t, 3, eh]
            for b in range(NV):
                at = eh * 128 + b * 8
                bs = pl.ds(b * 8, 8)
                iy = (b % 8) * 8 + 64 * eh
                f = plane[at:at + 8]
                shakhov = gauss * b_terms[t, 0, bs, :] * (
                    1.0 + (warm + b_terms[t, 1, bs, :]) * (shape + b_terms[t, 2, bs, :])
                )
                new = f * (keep - b_terms[t, 3, bs, :]) + shakhov
                new = new + speed * xs[at:at + 8]
                new = new + (DT * abs(node(b))) * ys[b // 8][iy:iy + 8]
                new = new + e_speed * zs[eh][b * 8:b * 8 + 8]
                rows.append(jnp.where(live, new, 0.0))
        return jnp.concatenate(rows, 0)

    def load(ref, p):
        return jnp.concatenate([ref[p, :, eh].reshape(128, 256) for eh in range(2)], 0)

    def store(ref, p, new):
        for eh in range(2):
            ref[p, :, eh] = new[eh * 128:eh * 128 + 128].reshape(16, 8, 256)

    meta[x] = meta_in[...]
    matrices(x)

    def first_send(p, carry):
        send_plane(0, x, p, load(dist, x * half + p))
        return carry

    lax.fori_loop(0, half, first_send, 0)
    acc[...] = jnp.zeros_like(acc)

    def first_moments(p, carry):
        add_moments(x, base + p, load(dist, p))
        return carry

    lax.fori_loop(0, planes, first_moments, 0)
    reduce_moments(0, x)
    part[0, other] = jnp.zeros((16, 256), F32)
    for k in range(1, 2 * n_vel):
        part_copy(0, k).start()
    acc[...] = jnp.zeros_like(acc)

    def rest_of_bulk(p, carry):
        bulk_copy(p).start()
        return carry

    lax.fori_loop(1, half, rest_of_bulk, 0)
    meta_copy.wait()
    matrices(other)

    for t in range(2):
        for g in range(4):
            inside, _, _ = block(t, OFFSETS[g])

            @pl.when(jnp.logical_not(inside))
            def _(t=t, g=g):
                for s in range(STEPS):
                    def clear(p, carry):
                        recv_buf[s, t, p, g] = jnp.zeros((128, 128), F32)
                        return carry
                    lax.fori_loop(0, half, clear, 0)

    for k in range(1, 2 * n_vel):
        part_copy(0, k).wait()

    def both_terms(s):
        def one(t, carry):
            terms(s, t)
            return carry
        lax.fori_loop(0, 2, one, 0)

    both_terms(0)

    def first_advance(t, p, plane):
        new = advance_plane(0, t, p, plane)
        send_plane(1, t, p, new)
        state1[t, p] = new
        add_moments(t, first_a + p, new)

    def first_step(p, carry):
        @pl.when(p < half)
        def _():
            bulk_copy(p).wait_recv()
            send_plane(0, other, p, load(bulk, p))

        @pl.when(p > 0)
        def _():
            first_advance(x, p - 1, load(dist, x * half + p - 1))
            first_advance(other, p - 1, load(bulk, p - 1))
        return carry

    lax.fori_loop(0, half + 1, first_step, 0)

    def both_reduce(t, carry):
        reduce_moments(1, t)
        return carry

    lax.fori_loop(0, 2, both_reduce, 0)
    for k in range(1, 2 * n_vel):
        part_copy(1, k).start()
    for k in range(1, 2 * n_vel):
        part_copy(1, k).wait()
    both_terms(1)

    def second_other(p, carry):
        store(out_buf, p, advance_plane(1, other, p, state1[other, p]))
        out_copy(p).start()
        return carry

    lax.fori_loop(0, half, second_other, 0)

    def second_own(p, carry):
        store(out, x * half + p, advance_plane(1, x, p, state1[x, p]))
        return carry

    lax.fori_loop(0, half, second_own, 0)

    def drain(p, carry):
        bulk_copy(p).wait_send()
        for s in range(STEPS):
            for t in range(2):
                for j in range(4):
                    if (t, j) not in ((1, 0), (0, 3)):
                        inside, _, _ = block(t, OFFSETS[j])

                        @pl.when(inside)
                        def _(s=s, t=t, j=j):
                            message(s, t, p, j).wait_send()
        out_copy(p).wait()
        return carry

    lax.fori_loop(0, half, drain, 0)


def solution(mesh):
    n_cell, n_vel = mesh.shape["cell"], mesh.shape["vel"]

    def body(distribution, cell_count, cell_level, send_list, face_neighbour, face_level):
        rows, width = distribution.shape
        planes = rows // (NV * NV)
        shape = (planes, NV, 2, NV // 2, width)
        half = planes // 2
        vmem = pl.BlockSpec(memory_space=pltpu.VMEM)
        meta = jnp.concatenate([
            face_neighbour, face_level, cell_level.reshape(1, width), send_list.reshape(1, width),
            jnp.broadcast_to(cell_count.reshape(1, 1), (2, width)),
        ], 0)
        result = pl.pallas_call(
            functools.partial(kernel, n_cell, n_vel, planes),
            out_shape=jax.ShapeDtypeStruct(shape, F32),
            in_specs=[vmem, vmem],
            out_specs=vmem,
            scratch_shapes=[
                pltpu.VMEM((2, 16, 256), jnp.int32),
                pltpu.VMEM((half, NV, 2, NV // 2, width), F32),
                pltpu.VMEM((half, NV, 2, NV // 2, width), F32),
                pltpu.VMEM((2, half, 256, 256), F32),
                pltpu.VMEM((STEPS, 2, half, 4, 128, 128), F32),
                pltpu.VMEM((STEPS, 2, half, 4, 128, 128), F32),
                pltpu.VMEM((2, 256, 256), BF16),
                pltpu.VMEM((2, 5, 512, 256), BF16),
                pltpu.VMEM((2, 4, 256, 256), F32),
                pltpu.VMEM((STEPS, 2, 16, 256), F32),
                pltpu.VMEM((STEPS, 2 * n_vel, 2, 16, 256), F32),
                pltpu.VMEM((2, 4, 128, 256), F32),
                pltpu.VMEM((2, 4, 2, 8, 256), F32),
                pltpu.VMEM((2, 5, 8, 256), F32),
                pltpu.VMEM((2, 6, 8, 256), F32),
                pltpu.SemaphoreType.DMA((STEPS, 2, half, 4)),
                pltpu.SemaphoreType.DMA((STEPS, 2, half, 4)),
                pltpu.SemaphoreType.DMA((STEPS, 2 * n_vel)),
                pltpu.SemaphoreType.DMA((STEPS, 2 * n_vel)),
                pltpu.SemaphoreType.DMA((half,)),
                pltpu.SemaphoreType.DMA((half,)),
                pltpu.SemaphoreType.DMA((half,)),
                pltpu.SemaphoreType.DMA((half,)),
                pltpu.SemaphoreType.DMA,
                pltpu.SemaphoreType.DMA,
            ],
            compiler_params=pltpu.CompilerParams(
                collective_id=0, has_side_effects=True, vmem_limit_bytes=48 * 2**20
            ),
        )(distribution.reshape(shape), meta)
        return result.reshape(rows, width)

    placed = (P("vel", "cell"), P("cell"), P("cell"), P(None, "cell"), P(None, "cell"), P(None, "cell"))
    return jax.shard_map(body, mesh=mesh, in_specs=placed, out_specs=P("vel", "cell"), check_vma=False)
```
